128 devices in a mesh: gz: 16 (over y, z), ta: 8 (over x, core).
Axes of the slice: x: 4, y: 4, z: 4, core: 2. Of those that a mesh axis runs over, the one named last changes fastest.
Arguments:
- potential: float32 [128, 128, 128, 128], P('ta', 'gz'), may hold values from -6 to 6
Outputs:
- propagator: float32 [128, 128, 128, 128], P('ta', 'gz')
The draws below stay inside these ranges and needn't reach their ends.
All inputs are finite; a program needn't handle non-finite values.
Results may differ from the reference program's by a relative error of at most 0.000071.
Values sent between devices are 32-bit elements; how exact they have to be, the bound alone decides.
No kernel may reach another device: no remote copies, remote signals or barrier semaphores. Data moves between devices by JAX's collectives and lax.ppermute only.
A program may use at most 128 MiB of HBM per device.

```python
import jax
import jax.numpy as jnp
from jax import lax

LX = 128
LY = 128
LZ = 128
LT = 128


def block_scale(rng, extent, pieces, smallest, high):
    def one(axis_at, blocks):
        steps = jax.random.uniform(jax.random.fold_in(jax.random.fold_in(rng, 6), axis_at), (blocks,), jnp.float32, smallest / len(pieces), high / len(pieces))
        return jnp.repeat(jnp.exp(steps), extent[axis_at] // blocks).reshape((-1,) + (1,) * (len(extent) - axis_at - 1))

    level = one(*pieces[0])
    for cut in pieces[1:]:
        level = level * one(*cut)
    return level


def bell_draw(key, extent, spread, limit, split=(), held_as=jnp.bfloat16):
    loudness = block_scale(key, extent, split, -0.22, 0.18) if split else 1.0
    array = jax.random.normal(key, extent, jnp.float32) * spread * loudness
    return jnp.minimum(jnp.maximum(array, -limit), limit).astype(held_as)


def setup_inputs(seed: int = 0) -> dict:
    arg_keys = jax.random.split(jax.random.key(seed), 2)
    potential = bell_draw(arg_keys[0], (LT, LZ, LY, LX), 1.0, 6.0, ((0, 8), (1, 16)), jnp.float32)
    return {"potential": potential}


def reference(potential):
    def slab(piece):
        spectrum = jnp.fft.fftn(piece, norm="ortho")
        return spectrum.real, spectrum.imag

    real_part, imag_part = lax.map(slab, potential)

    def column(index):
        column_re = lax.dynamic_index_in_dim(real_part, index, 1, keepdims=False)
        column_im = lax.dynamic_index_in_dim(imag_part, index, 1, keepdims=False)
        spectrum = jnp.fft.fft(column_re + 1j * column_im, axis=0, norm="ortho")
        return spectrum.real * spectrum.real + spectrum.imag * spectrum.imag

    power = lax.map(column, jnp.arange(LZ, dtype=jnp.int32))
    return jnp.transpose(power, (1, 0, 2, 3))
```

```python
import math

import ml_dtypes
import numpy as np

import jax
import jax.numpy as jnp
from jax import lax
from jax.experimental import pallas as pl
from jax.experimental.pallas import tpu as pltpu
from jax.sharding import PartitionSpec as P

N = 128
H = 64
AXES = ("gz", "ta")
BF = jnp.bfloat16
F32 = jnp.float32


def split_np(w):
    hi = w.astype(ml_dtypes.bfloat16)
    lo = (w - hi.astype(np.float64)).astype(ml_dtypes.bfloat16)
    return hi, lo


def angles():
    k = np.arange(N)
    phase = np.outer(k, k) % N
    c = np.cos(2 * np.pi * phase / N)
    s = np.sin(2 * np.pi * phase / N)
    quarter = phase % (N // 4) == 0
    c[quarter] = np.round(c[quarter])
    s[quarter] = np.round(s[quarter])
    return c, s


def table_x():
    c, s = angles()
    w = np.concatenate([c[:, :H], -s[:, :H]], axis=1)
    w[:, H] = c[:, H]
    hi, lo = split_np(w / N)
    row = np.concatenate([hi, lo], axis=1)
    return np.concatenate([row, row], axis=0)


def table_full(scale):
    c, s = angles()
    hi, lo = split_np(np.concatenate([c, s], axis=0) * scale)
    hi = np.concatenate([hi, hi], axis=1)
    lo = np.concatenate([lo, lo], axis=1)
    return np.concatenate([hi, lo], axis=0)


def split(x):
    hi = x.astype(BF)
    lo = (x - hi.astype(F32)).astype(BF)
    return hi, lo


def stacked(parts):
    his, los = zip(*[split(p) for p in parts])
    return jnp.concatenate([jnp.concatenate(his, axis=1), jnp.concatenate(los, axis=1)], axis=0)


def cos_sin(table, parts):
    out = jnp.dot(table, stacked(parts), preferred_element_type=F32)
    rows = table.shape[0] // 2
    out = out[:rows] + out[rows:]
    half = rows // 2
    return [(out[:half, N * i : N * i + N], out[half:, N * i : N * i + N]) for i in range(2)]


def lane_of(shape):
    return lax.broadcasted_iota(jnp.int32, shape, 1)


def xy_kernel(x_ref, wx_ref, wy_ref, o_ref):
    planes = x_ref.shape[1]
    x = x_ref[0].reshape(planes * N, N)
    hi, lo = split(x)
    r = jnp.dot(jnp.concatenate([hi, lo], axis=1), wx_ref[...], preferred_element_type=F32)
    r = r[:, :N] + r[:, N:]
    lane = lane_of((N, N))
    row = lax.broadcasted_iota(jnp.int32, (N, N), 0)
    late = row > H
    sign = jnp.where(lane < H, 1.0, -1.0).astype(F32)
    swap = (lane == H) & late
    keep = jnp.where((lane == 0) & late, 0.0, jnp.where((lane == H) & (row % H != 0), 0.0, 1.0)).astype(F32)
    roll = jnp.where((lane == 0) & ~late, 0.0, sign).astype(F32)
    for z in range(0, planes, 2):
        for i, (p, q) in enumerate(cos_sin(wy_ref[...], [r[N * z : N * z + N], r[N * z + N : N * z + 2 * N]])):
            turned = pltpu.roll(jnp.where(swap, p, q), H, 1)
            a = jnp.where(swap, -q, p * keep + turned * roll)
            o_ref[:, 0, z + i, :] = a


def xy_transform(potential):
    t, z, _, _ = potential.shape
    return pl.pallas_call(
        xy_kernel,
        grid=(t,),
        in_specs=[
            pl.BlockSpec((1, z, N, N), lambda i: (i, 0, 0, 0)),
            pl.BlockSpec((2 * N, 2 * N), lambda i: (0, 0)),
            pl.BlockSpec((4 * N, 2 * N), lambda i: (0, 0)),
        ],
        out_specs=pl.BlockSpec((N, 1, z, N), lambda i: (0, i, 0, 0)),
        out_shape=jax.ShapeDtypeStruct((N, t, z, N), F32),
        compiler_params=pltpu.CompilerParams(vmem_limit_bytes=40 * 2**20),
    )(potential, jnp.asarray(table_x()), jnp.asarray(table_full(1.0)))


def z_kernel(x_ref, w_ref, o_ref):
    g, _, rows, z, _ = x_ref.shape
    sign = jnp.where(lane_of((N, N)) < H, 1.0, -1.0).astype(F32)
    for t in range(0, rows, 2):
        parts = [x_ref[:, 0, t + i].reshape(g * z, N) for i in range(2)]
        for i, (p, q) in enumerate(cos_sin(w_ref[...], parts)):
            o_ref[:, 0, t + i, :] = p + pltpu.roll(q, H, 1) * sign


def z_transform(field, gz, ta):
    _, t, z, _ = field.shape
    field = field.reshape(gz, ta, t, z, N)
    return pl.pallas_call(
        z_kernel,
        grid=(ta,),
        in_specs=[
            pl.BlockSpec((gz, 1, t, z, N), lambda i: (0, i, 0, 0, 0)),
            pl.BlockSpec((4 * N, 2 * N), lambda i: (0, 0)),
        ],
        out_specs=pl.BlockSpec((N, 1, t, N), lambda i: (0, i, 0, 0)),
        out_shape=jax.ShapeDtypeStruct((N, ta, t, N), F32),
        compiler_params=pltpu.CompilerParams(vmem_limit_bytes=40 * 2**20),
    )(field, jnp.asarray(table_full(1.0 / N)))


def t_kernel(y_ref, w_ref, o_ref):
    gz, _, planes, _ = o_ref.shape
    me = lax.axis_index("gz") * lax.axis_size("ta") + lax.axis_index("ta")
    lane = lane_of((N, N))
    sign = jnp.where(lane < H, 1.0, -1.0).astype(F32)
    edge = (lane == 0) | (lane == H)
    own = edge & ((me == 0) | (me == H))
    late = edge & (me > H)
    first = (lane < H) ^ late
    same = jnp.where(own, 0.5, 1.0).astype(F32)
    mixed = jnp.where(own, 0.5 * sign, 0.0).astype(F32)
    same_b = jnp.where(own, -0.5 * sign, 1.0).astype(F32)
    mixed_b = jnp.where(own, 0.5, 0.0).astype(F32)

    def power(plus, minus):
        a = plus * same + minus * mixed
        b = plus * mixed_b + minus * same_b
        a = a * a
        b = b * b
        return jnp.where(first, a, b) + pltpu.roll(jnp.where(first, b, a), H, 1)

    def step(g, carry):
        for j in range(planes):
            kz = g * planes + j
            other = jnp.where(kz == 0, N // 2, N - kz)
            parts = [y_ref[kz], y_ref[other]]
            (pa, qa), (pb, qb) = cos_sin(w_ref[...], parts)
            qa = pltpu.roll(qa, H, 1) * sign
            qb = pltpu.roll(qb, H, 1) * sign
            minus_a, minus_b = pa - qa, pb - qb
            if j == 0:
                alone = g == 0
                minus_a, minus_b = jnp.where(alone, minus_b, minus_a), jnp.where(alone, minus_a, minus_b)
                there = jnp.where(alone, gz // 2, gz - g)
                slot = 0
            else:
                there = gz - 1 - g
                slot = planes - j
            o_ref[g, :, j, :] = power(pa + qa, minus_b)
            o_ref[there, :, slot, :] = power(pb + qb, minus_a)
        return carry

    lax.fori_loop(0, gz // 2, step, 0)


def t_transform(y, gz, planes):
    return pl.pallas_call(
        t_kernel,
        in_specs=[pl.BlockSpec(memory_space=pltpu.VMEM)] * 2,
        out_specs=pl.BlockSpec(memory_space=pltpu.VMEM),
        out_shape=jax.ShapeDtypeStruct((gz, N, planes, N), F32),
        compiler_params=pltpu.CompilerParams(vmem_limit_bytes=40 * 2**20),
    )(y.reshape(N, N, N), jnp.asarray(table_full(1.0)))


def join_kernel(x_ref, o_ref):
    z = x_ref.shape[2]
    lane = lane_of((z, N))
    back = (N + H - lane) % N
    for s in range(N):
        here = x_ref[s, 0]
        there = jnp.take_along_axis(x_ref[(N - s) % N, 0], back, axis=1)
        if s == 0 or s == H:
            mine = lane <= H
        elif s < H:
            mine = lane < H
        else:
            mine = (lane <= H) & (lane > 0)
        o_ref[0, :, s, :] = jnp.where(mine, here, there)


def join(received):
    _, t, z, _ = received.shape
    return pl.pallas_call(
        join_kernel,
        grid=(t,),
        in_specs=[pl.BlockSpec((N, 1, z, N), lambda i: (0, i, 0, 0))],
        out_specs=pl.BlockSpec((1, z, N, N), lambda i: (i, 0, 0, 0)),
        out_shape=jax.ShapeDtypeStruct((t, z, N, N), F32),
        compiler_params=pltpu.CompilerParams(vmem_limit_bytes=40 * 2**20),
    )(received)


def body(potential):
    t, z, _, _ = potential.shape
    gz = lax.axis_size("gz")
    ta = lax.axis_size("ta")
    sent = xy_transform(potential)
    field = lax.all_to_all(sent, AXES, split_axis=0, concat_axis=0, tiled=True)
    y = z_transform(field, gz, ta)
    power = t_transform(y, gz, z)
    power = power.reshape(gz * ta, t, z, N)
    received = lax.all_to_all(power, AXES, split_axis=0, concat_axis=0, tiled=True)
    return join(received)


def solution(mesh):
    return jax.shard_map(
        body,
        mesh=mesh,
        in_specs=(P("ta", "gz", None, None),),
        out_specs=P("ta", "gz", None, None),
        check_vma=False,
    )
```

```python
import ml_dtypes
import numpy as np

import jax
import jax.numpy as jnp
from jax import lax
from jax.experimental import pallas as pl
from jax.experimental.pallas import tpu as pltpu
from jax.sharding import PartitionSpec as P

N = 128
H = 64
AXES = ("gz", "ta")
BF = jnp.bfloat16
F32 = jnp.float32
MIB = 2**20
ROOT = float(np.sqrt(0.5))


def split_np(w):
    hi = w.astype(ml_dtypes.bfloat16)
    lo = (w - hi.astype(np.float64)).astype(ml_dtypes.bfloat16)
    return hi, lo


def angles():
    k = np.arange(N)
    phase = np.outer(k, k) % N
    c = np.cos(2 * np.pi * phase / N)
    s = np.sin(2 * np.pi * phase / N)
    quarter = phase % (N // 4) == 0
    c[quarter] = np.round(c[quarter])
    s[quarter] = np.round(s[quarter])
    return c, s


def table_x():
    c, s = angles()
    w = np.concatenate([c[:, :H], -s[:, :H]], axis=1)
    w[:, H] = c[:, H]
    hi, lo = split_np(w / N)
    row = np.concatenate([hi, lo], axis=1)
    return np.concatenate([row, row], axis=0)


def table_z():
    c, s = angles()
    hi, lo = split_np(np.concatenate([c[: H + 1], s[1:H]], axis=0) / N)
    return np.concatenate([hi, hi, lo, lo], axis=1)


def split(x):
    hi = x.astype(BF)
    lo = (x - hi.astype(F32)).astype(BF)
    return hi, lo


def add(a, b):
    im = b[1] if a[1] is None else a[1] if b[1] is None else a[1] + b[1]
    return a[0] + b[0], im


def sub(a, b):
    im = a[1] if b[1] is None else -b[1] if a[1] is None else a[1] - b[1]
    return a[0] - b[0], im


def conj(a):
    return a[0], None if a[1] is None else -a[1]


def turn_by(a, k, n):
    k = k % n
    re, im = a
    if k == 0:
        return a
    if 4 * k == n:
        return jnp.zeros_like(re) if im is None else im, -re
    if im is None:
        angle = 2 * np.pi * k / n
        return re * float(np.cos(angle)), re * float(-np.sin(angle))
    if 8 * k == n:
        return (re + im) * ROOT, (im - re) * ROOT
    if 8 * k == 3 * n:
        return (im - re) * ROOT, (re + im) * -ROOT
    c, s = float(np.cos(2 * np.pi * k / n)), float(np.sin(2 * np.pi * k / n))
    return re * c + im * s, im * c - re * s


def transform(x):
    n = len(x)
    if n == 1:
        return x
    even, odd = transform(x[0::2]), transform(x[1::2])
    out = [None] * n
    for k in range(n // 2):
        t = turn_by(odd[k], k, n)
        out[k], out[k + n // 2] = add(even[k], t), sub(even[k], t)
    return out


def transform_real(x):
    n = len(x)
    if n == 1:
        return [(x[0], None)]
    if n == 2:
        return [(x[0] + x[1], None), (x[0] - x[1], None)]
    even, odd = transform_real(x[0::2]), transform_real(x[1::2])
    out = [None] * (n // 2 + 1)
    out[0], out[n // 2] = add(even[0], odd[0]), sub(even[0], odd[0])
    for k in range(1, n // 4):
        t = turn_by(odd[k], k, n)
        out[k], out[n // 2 - k] = add(even[k], t), conj(sub(even[k], t))
    out[n // 4] = (even[n // 4][0], -odd[n // 4][0])
    return out


def lane_of(shape):
    return lax.broadcasted_iota(jnp.int32, shape, 1)


def xy_kernel(x_ref, w_ref, o_ref, x_buf, f_buf, h_buf, x_sem):
    steps, planes = x_ref.shape[:2]
    slots = x_buf.shape[0]
    lane = lane_of((planes, N))
    keep = jnp.where(lane == H, 0.0, 1.0).astype(F32)
    turn = jnp.where(lane == 0, 0.0, jnp.where(lane < H, -1.0, 1.0)).astype(F32)
    keep_back = jnp.where(lane == 0, 0.0, 1.0).astype(F32)
    turn_back = jnp.where(lane < H, 1.0, -1.0).astype(F32)
    edge = lane == H

    def fetch(t, slot):
        return [
            pltpu.make_async_copy(x_ref.at[t, z], x_buf.at[slot, :, z, :], x_sem.at[slot, z])
            for z in range(planes)
        ]

    for t in range(slots):
        for copy in fetch(t, t):
            copy.start()

    def step(t, carry):
        slot = lax.rem(t, slots)
        for copy in fetch(t, slot):
            copy.wait()
        for b in range(8):
            for c, v in enumerate(transform_real([x_buf[slot, 8 * a + b] for a in range(16)])):
                re, im = turn_by(v, b * c, N)
                h_buf[0, c, b] = re
                if im is not None:
                    h_buf[1, c, b] = im
        for c in range(9):
            real = c == 0
            parts = []
            for b in range(8):
                flat = real or (c == 8 and b == 0)
                parts.append((h_buf[0, c, b], None if flat else h_buf[1, c, b]))
            if real:
                parts = transform_real([v[0] for v in parts])
            else:
                parts = transform(parts)
            for d, v in enumerate(parts):
                ky = c + 16 * d
                if c == 8 and d >= 4:
                    continue
                re, im = v
                if ky > H:
                    ky, im = N - ky, -im
                f_buf[ky] = re
                if ky % H:
                    f_buf[H + ky] = im

        @pl.when(t + slots < steps)
        def _():
            for copy in fetch(t + slots, slot):
                copy.start()

        hi, lo = split(f_buf[...].reshape(N * planes, N))
        r = jnp.dot(jnp.concatenate([hi, lo], axis=1), w_ref[...], preferred_element_type=F32)
        r = (r[:, :N] + r[:, N:]).reshape(N, planes, N)
        o_ref[0, t] = r[0]
        o_ref[H, t] = r[H]
        for i in range(1, H):
            p, q = r[i], r[H + i]
            turned = pltpu.roll(jnp.where(edge, p, q), H, 1)
            o_ref[i, t] = p * keep + turned * turn
            o_ref[H + i, t] = jnp.where(edge, -q, p * keep_back + turned * turn_back)
        return carry

    lax.fori_loop(0, steps, step, 0)


def xy_transform(potential):
    t, z, _, _ = potential.shape
    slots = 6
    return pl.pallas_call(
        xy_kernel,
        in_specs=[pl.BlockSpec(memory_space=pltpu.HBM), pl.BlockSpec(memory_space=pltpu.VMEM)],
        out_specs=pl.BlockSpec(memory_space=pltpu.VMEM),
        out_shape=jax.ShapeDtypeStruct((N, t, z, N), F32),
        scratch_shapes=[
            pltpu.VMEM((slots, N, z, N), F32),
            pltpu.VMEM((N, z, N), F32),
            pltpu.VMEM((2, 9, 8, z, N), F32),
            pltpu.SemaphoreType.DMA((slots, z)),
        ],
        compiler_params=pltpu.CompilerParams(vmem_limit_bytes=48 * MIB),
    )(potential, jnp.asarray(table_x()))


def zt_kernel(x_ref, w_ref, o_ref, y_ref):
    gz, times, planes, _ = x_ref.shape
    groups = gz // 2
    me = lax.axis_index("gz") * lax.axis_size("ta") + lax.axis_index("ta")
    lane = lane_of((1, N))
    first = lane < H
    paired = (me == 0) | (me == H)
    late = me > H
    low, high = lane == 0, lane == H
    u_p = jnp.where(high & late, -1.0, 1.0).astype(F32)
    u_q = jnp.where((low | high) & paired, 0.0, jnp.where(low & late, -1.0, 1.0)).astype(F32)
    v_p = jnp.where((low | high) & paired, 0.0, jnp.where(low & late, -1.0, 1.0)).astype(F32)
    v_q = jnp.where(high & (paired | late), -1.0, 1.0).astype(F32)
    flip = jnp.where((low | high) & late, -1.0, 1.0).astype(F32)
    top = lax.broadcasted_iota(jnp.int32, (planes, N), 0) == 0
    first_8 = lane_of((planes, N)) < H
    edge_8 = (lane_of((planes, N)) == 0) | (lane_of((planes, N)) == H)
    own_8 = edge_8 & paired
    own_top = own_8 & top
    straight = first_8 | own_8

    def z_step(n, carry):
        for m in range(0, 8, 2):
            his, los = zip(*[split(x_ref[:, 8 * n + m + i].reshape(gz * planes, N)) for i in range(2)])
            hi, lo = jnp.concatenate(his, axis=1), jnp.concatenate(los, axis=1)
            out = jnp.dot(w_ref[...], jnp.concatenate([hi, lo, hi, lo], axis=0), preferred_element_type=F32)
            for i in range(2):
                t = 8 * n + m + i
                p, q = out[:H, N * i : N * i + N], out[H:, N * i : N * i + N]
                rp, rq = pltpu.roll(p, H, 1), pltpu.roll(q, H, 1)
                u, v = p * u_p + rq * u_q, rp * v_p - q * v_q
                re, im = jnp.where(first, u, v), jnp.where(first, v, u)
                y_ref[0, :, t] = re.reshape(groups, planes, N)
                y_ref[1, :, t] = im.reshape(groups, planes, N)
                re_0 = jnp.where(first_8, p[:planes], rq[:planes])
                im_0 = jnp.where(first_8, rp[:planes], q[:planes]) * flip
                y_ref[0, 0, t] = jnp.where(top, re_0, re[:planes])
                y_ref[1, 0, t] = jnp.where(top, im_0, im[:planes])
        return carry

    lax.fori_loop(0, times // 8, z_step, 0)

    def t_group(g, lowest):
        for b in range(8):
            parts = transform([(y_ref[0, g, 8 * a + b], y_ref[1, g, 8 * a + b]) for a in range(16)])
            for c, v in enumerate(parts):
                re, im = turn_by(v, b * c, N)
                y_ref[0, g, 8 * c + b] = re
                y_ref[1, g, 8 * c + b] = im
        for c in range(9):
            spectrum = {}
            for k in {c, (16 - c) % 16}:
                parts = transform([(y_ref[0, g, 8 * k + b], y_ref[1, g, 8 * k + b]) for b in range(8)])
                for d, v in enumerate(parts):
                    spectrum[k + 16 * d] = v
            power = {k: re * re + im * im for k, (re, im) in spectrum.items()}
            for k in spectrum:
                ahead, back = power[k], power[(N - k) % N]
                here = jnp.where(straight, ahead, back)
                there = jnp.where(own_8, back, pltpu.roll(jnp.where(first_8, back, ahead), H, 1))
                if lowest:
                    upper = top & ~first_8
                    here, there = jnp.where(upper, there, here), jnp.where(upper, here, there)
                    (re, im), (re_m, im_m) = spectrum[k], spectrum[(N - k) % N]
                    one = (re + re_m) * (re + re_m) + (im - im_m) * (im - im_m)
                    two = (im + im_m) * (im + im_m) + (re - re_m) * (re - re_m)
                    one, two = one * 0.25, two * 0.25
                    mixed = jnp.where(first_8, two, one)
                    mixed = pltpu.roll(mixed, H, 1)
                    here = jnp.where(own_top, jnp.where(first_8, one, mixed), here)
                    there = jnp.where(own_top, jnp.where(first_8, mixed, two), there)
                o_ref[g, k] = here
                o_ref[gz - 1 - g, k, 1:, :] = there[1:]
                o_ref[groups if lowest else gz - g, k, :1, :] = there[:1]

    t_group(0, True)

    def t_step(g, carry):
        t_group(g, False)
        return carry

    lax.fori_loop(1, groups, t_step, 0)


def zt_transform(field, gz, ta):
    _, t, z, _ = field.shape
    field = field.reshape(gz, ta * t, z, N)
    return pl.pallas_call(
        zt_kernel,
        in_specs=[pl.BlockSpec(memory_space=pltpu.VMEM)] * 2,
        out_specs=pl.BlockSpec(memory_space=pltpu.VMEM),
        out_shape=jax.ShapeDtypeStruct((gz, N, z, N), F32),
        scratch_shapes=[pltpu.VMEM((2, gz // 2, N, z, N), F32)],
        compiler_params=pltpu.CompilerParams(vmem_limit_bytes=36 * MIB),
    )(field, jnp.asarray(table_z()))


def join_kernel(x_ref, o_ref, o_buf, o_sem):
    steps, z = o_ref.shape[:2]
    slots = o_buf.shape[0]
    falling = lax.axis_index("gz") >= lax.axis_size("gz") // 2
    lane = lane_of((z, N))
    back = (N + H - lane) % N

    def flush(t, slot):
        return [
            pltpu.make_async_copy(
                o_buf.at[slot, :, r, :],
                o_ref.at[t, jnp.where(falling, (z - r) % z, r)],
                o_sem.at[slot, r],
            )
            for r in range(z)
        ]

    def step(t, carry):
        slot = lax.rem(t, slots)

        @pl.when(t >= slots)
        def _():
            for copy in flush(t - slots, slot):
                copy.wait()

        for i in range(H):
            a, b = x_ref[i, t], x_ref[H + i, t]
            back_a = jnp.take_along_axis(a, back, axis=1)
            back_b = jnp.take_along_axis(b, back, axis=1)
            if i == 0:
                o_buf[slot, 0] = jnp.where(lane <= H, a, back_a)
                o_buf[slot, H] = jnp.where(lane <= H, b, back_b)
            else:
                o_buf[slot, i] = jnp.where(lane < H, a, back_b)
                o_buf[slot, N - i] = jnp.where((lane <= H) & (lane > 0), b, back_a)
        for copy in flush(t, slot):
            copy.start()
        return carry

    lax.fori_loop(0, steps, step, 0)
    for t in range(steps - slots, steps):
        for copy in flush(t, t % slots):
            copy.wait()


def join(received):
    _, t, z, _ = received.shape
    slots = 4
    return pl.pallas_call(
        join_kernel,
        in_specs=[pl.BlockSpec(memory_space=pltpu.VMEM)],
        out_specs=pl.BlockSpec(memory_space=pltpu.HBM),
        out_shape=jax.ShapeDtypeStruct((t, z, N, N), F32),
        scratch_shapes=[pltpu.VMEM((slots, N, z, N), F32), pltpu.SemaphoreType.DMA((slots, z))],
        compiler_params=pltpu.CompilerParams(vmem_limit_bytes=20 * MIB),
    )(received)


def body(potential):
    t, z, _, _ = potential.shape
    gz = lax.axis_size("gz")
    ta = lax.axis_size("ta")
    sent = xy_transform(potential)
    field = lax.all_to_all(sent, AXES, split_axis=0, concat_axis=0, tiled=True)
    power = zt_transform(field, gz, ta).reshape(gz * ta, t, z, N)
    received = lax.all_to_all(power, AXES, split_axis=0, concat_axis=0, tiled=True)
    return join(received)


def solution(mesh):
    return jax.shard_map(
        body,
        mesh=mesh,
        in_specs=(P("ta", "gz", None, None),),
        out_specs=P("ta", "gz", None, None),
        check_vma=False,
    )
```

```python
import ml_dtypes
import numpy as np

import jax
import jax.numpy as jnp
from jax import lax
from jax.experimental import pallas as pl
from jax.experimental.pallas import tpu as pltpu
from jax.sharding import PartitionSpec as P

N = 128
H = 64
AXES = ("gz", "ta")
BF = jnp.bfloat16
F32 = jnp.float32
MIB = 2**20
ROOT = float(np.sqrt(0.5))


def split_np(w):
    hi = w.astype(ml_dtypes.bfloat16)
    lo = (w - hi.astype(np.float64)).astype(ml_dtypes.bfloat16)
    return hi, lo


def angles():
    k = np.arange(N)
    phase = np.outer(k, k) % N
    c = np.cos(2 * np.pi * phase / N)
    s = np.sin(2 * np.pi * phase / N)
    quarter = phase % (N // 4) == 0
    c[quarter] = np.round(c[quarter])
    s[quarter] = np.round(s[quarter])
    return c, s


def table_x():
    c, s = angles()
    w = np.concatenate([c[:, :H], -s[:, :H]], axis=1)
    w[:, H] = c[:, H]
    hi, lo = split_np(w / N)
    row = np.concatenate([hi, lo], axis=1)
    return np.concatenate([row, row], axis=0)


def table_z():
    c, s = angles()
    hi, lo = split_np(np.concatenate([c[: H + 1], s[1:H]], axis=0) / N)
    return np.concatenate([hi, hi, lo, lo], axis=1)


def split(x):
    hi = x.astype(BF)
    lo = (x - hi.astype(F32)).astype(BF)
    return hi, lo


def add(a, b):
    im = b[1] if a[1] is None else a[1] if b[1] is None else a[1] + b[1]
    return a[0] + b[0], im


def sub(a, b):
    im = a[1] if b[1] is None else -b[1] if a[1] is None else a[1] - b[1]
    return a[0] - b[0], im


def turn_by(a, k, n):
    k = k % n
    re, im = a
    if k == 0:
        return a
    if 4 * k == n:
        return jnp.zeros_like(re) if im is None else im, -re
    if im is None:
        angle = 2 * np.pi * k / n
        return re * float(np.cos(angle)), re * float(-np.sin(angle))
    if 8 * k == n:
        return (re + im) * ROOT, (im - re) * ROOT
    if 8 * k == 3 * n:
        return (im - re) * ROOT, (re + im) * -ROOT
    c, s = float(np.cos(2 * np.pi * k / n)), float(np.sin(2 * np.pi * k / n))
    return re * c + im * s, im * c - re * s


def butterfly(a, b, k, n):
    if 4 * k == n and b[1] is not None and a[1] is not None:
        return (a[0] + b[1], a[1] - b[0]), (a[0] - b[1], a[1] + b[0])
    t = turn_by(b, k, n)
    return add(a, t), sub(a, t)


def transform(x):
    n = len(x)
    if n == 1:
        return x
    even, odd = transform(x[0::2]), transform(x[1::2])
    out = [None] * n
    for k in range(n // 2):
        out[k], out[k + n // 2] = butterfly(even[k], odd[k], k, n)
    return out


def transform_real(x):
    n = len(x)
    if n == 1:
        return [(x[0], None)]
    if n == 2:
        return [(x[0] + x[1], None), (x[0] - x[1], None)]
    even, odd = transform_real(x[0::2]), transform_real(x[1::2])
    out = [None] * (n // 2 + 1)
    out[0], out[n // 2] = add(even[0], odd[0]), sub(even[0], odd[0])
    for k in range(1, n // 4):
        (re, im), t = even[k], turn_by(odd[k], k, n)
        out[k], out[n // 2 - k] = (re + t[0], im + t[1]), (re - t[0], t[1] - im)
    out[n // 4] = (even[n // 4][0], -odd[n // 4][0])
    return out


def lane_of(shape):
    return lax.broadcasted_iota(jnp.int32, shape, 1)


def xy_kernel(x_ref, w_ref, o_ref, x_buf, f_buf, h_buf, x_sem):
    steps, planes = x_ref.shape[:2]
    lane = lane_of((planes, N))
    keep = jnp.where(lane == H, 0.0, 1.0).astype(F32)
    turn = jnp.where(lane == 0, 0.0, jnp.where(lane < H, -1.0, 1.0)).astype(F32)
    keep_back = jnp.where(lane == 0, 0.0, 1.0).astype(F32)
    turn_back = jnp.where(lane < H, 1.0, -1.0).astype(F32)
    edge = lane == H

    def fetch(n):
        for z in range(planes):
            pltpu.make_async_copy(
                x_ref.at[pl.ds(2 * n, 2), z], x_buf.at[pl.ds(2 * n, 2), :, z, :], x_sem.at[n]
            ).start()

    for n in range(2):
        fetch(n)

    def step(n, carry):
        @pl.when(n + 2 < steps // 2)
        def _():
            fetch(n + 2)

        whole = x_buf.at[pl.ds(2 * n, 2)]
        pltpu.make_async_copy(whole, whole, x_sem.at[n]).wait()
        for i in range(2):
            plane(2 * n + i)
        return carry

    def plane(t):
        for b in range(8):
            for c, v in enumerate(transform_real([x_buf[t, 8 * a + b] for a in range(16)])):
                re, im = turn_by(v, b * c, N)
                h_buf[0, c, b] = re
                if im is not None:
                    h_buf[1, c, b] = im
        for c in range(9):
            real = c == 0
            parts = []
            for b in range(8):
                flat = real or (c == 8 and b == 0)
                parts.append((h_buf[0, c, b], None if flat else h_buf[1, c, b]))
            if real:
                parts = transform_real([v[0] for v in parts])
            else:
                parts = transform(parts)
            for d, v in enumerate(parts):
                ky = c + 16 * d
                if c == 8 and d >= 4:
                    continue
                re, im = v
                if ky > H:
                    ky, im = N - ky, -im
                f_buf[ky] = re
                if ky % H:
                    f_buf[H + ky] = im

        hi, lo = split(f_buf[...].reshape(N * planes, N))
        r = jnp.dot(jnp.concatenate([hi, lo], axis=1), w_ref[...], preferred_element_type=F32)
        r = (r[:, :N] + r[:, N:]).reshape(N, planes, N)
        o_ref[0, t] = r[0]
        o_ref[H, t] = r[H]
        for i in range(1, H):
            p, q = r[i], r[H + i]
            turned = pltpu.roll(jnp.where(edge, p, q), H, 1)
            o_ref[i, t] = p * keep + turned * turn
            o_ref[H + i, t] = jnp.where(edge, -q, p * keep_back + turned * turn_back)

    lax.fori_loop(0, steps // 2, step, 0)


def xy_transform(potential):
    t, z, _, _ = potential.shape
    return pl.pallas_call(
        xy_kernel,
        in_specs=[pl.BlockSpec(memory_space=pltpu.HBM), pl.BlockSpec(memory_space=pltpu.VMEM)],
        out_specs=pl.BlockSpec(memory_space=pltpu.VMEM),
        out_shape=jax.ShapeDtypeStruct((N, t, z, N), F32),
        scratch_shapes=[
            pltpu.VMEM((t, N, z, N), F32),
            pltpu.VMEM((N, z, N), F32),
            pltpu.VMEM((2, 9, 8, z, N), F32),
            pltpu.SemaphoreType.DMA((t // 2,)),
        ],
        compiler_params=pltpu.CompilerParams(vmem_limit_bytes=42 * MIB),
    )(potential, jnp.asarray(table_x()))


def zt_kernel(x_ref, w_ref, o_ref, y_ref):
    gz, times, planes, _ = x_ref.shape
    groups = gz // 2
    me = lax.axis_index("gz") * lax.axis_size("ta") + lax.axis_index("ta")
    lane = lane_of((1, N))
    first = lane < H
    paired = (me == 0) | (me == H)
    late = me > H
    low, high = lane == 0, lane == H
    u_p = jnp.where(high & late, -1.0, 1.0).astype(F32)
    u_q = jnp.where((low | high) & paired, 0.0, jnp.where(low & late, -1.0, 1.0)).astype(F32)
    v_p = jnp.where((low | high) & paired, 0.0, jnp.where(low & late, -1.0, 1.0)).astype(F32)
    v_q = jnp.where(high & (paired | late), -1.0, 1.0).astype(F32)
    flip = jnp.where((low | high) & late, -1.0, 1.0).astype(F32)
    top = lax.broadcasted_iota(jnp.int32, (planes, N), 0) == 0
    first_8 = lane_of((planes, N)) < H
    edge_8 = (lane_of((planes, N)) == 0) | (lane_of((planes, N)) == H)
    own_8 = edge_8 & paired
    own_top = own_8 & top
    straight = first_8 | own_8

    def z_step(n, carry):
        for m in range(0, 32, 2):
            his, los = zip(*[split(x_ref[:, 32 * n + m + i].reshape(gz * planes, N)) for i in range(2)])
            hi, lo = jnp.concatenate(his, axis=1), jnp.concatenate(los, axis=1)
            out = jnp.dot(w_ref[...], jnp.concatenate([hi, lo, hi, lo], axis=0), preferred_element_type=F32)
            for i in range(2):
                t = 32 * n + m + i
                p, q = out[:H, N * i : N * i + N], out[H:, N * i : N * i + N]
                rp, rq = pltpu.roll(p, H, 1), pltpu.roll(q, H, 1)
                u, v = p * u_p + rq * u_q, rp * v_p - q * v_q
                re, im = jnp.where(first, u, v), jnp.where(first, v, u)
                y_ref[0, :, t] = re.reshape(groups, planes, N)
                y_ref[1, :, t] = im.reshape(groups, planes, N)
                re_0 = jnp.where(first_8, p[:planes], rq[:planes])
                im_0 = jnp.where(first_8, rp[:planes], q[:planes]) * flip
                y_ref[0, 0, t] = jnp.where(top, re_0, re[:planes])
                y_ref[1, 0, t] = jnp.where(top, im_0, im[:planes])
        return carry

    lax.fori_loop(0, times // 32, z_step, 0)

    def t_group(g, lowest):
        for b in range(8):
            parts = transform([(y_ref[0, g, 8 * a + b], y_ref[1, g, 8 * a + b]) for a in range(16)])
            for c, v in enumerate(parts):
                re, im = turn_by(v, b * c, N)
                y_ref[0, g, 8 * c + b] = re
                y_ref[1, g, 8 * c + b] = im
        for c in range(9):
            spectrum = {}
            for k in {c, (16 - c) % 16}:
                parts = transform([(y_ref[0, g, 8 * k + b], y_ref[1, g, 8 * k + b]) for b in range(8)])
                for d, v in enumerate(parts):
                    spectrum[k + 16 * d] = v
            power = {k: re * re + im * im for k, (re, im) in spectrum.items()}
            for k in spectrum:
                ahead, back = power[k], power[(N - k) % N]
                here = jnp.where(straight, ahead, back)
                there = jnp.where(own_8, back, pltpu.roll(jnp.where(first_8, back, ahead), H, 1))
                if lowest:
                    upper = top & ~first_8
                    here, there = jnp.where(upper, there, here), jnp.where(upper, here, there)
                    (re, im), (re_m, im_m) = spectrum[k], spectrum[(N - k) % N]
                    one = (re + re_m) * (re + re_m) + (im - im_m) * (im - im_m)
                    two = (im + im_m) * (im + im_m) + (re - re_m) * (re - re_m)
                    one, two = one * 0.25, two * 0.25
                    mixed = jnp.where(first_8, two, one)
                    mixed = pltpu.roll(mixed, H, 1)
                    here = jnp.where(own_top, jnp.where(first_8, one, mixed), here)
                    there = jnp.where(own_top, jnp.where(first_8, mixed, two), there)
                o_ref[g, k] = here
                o_ref[gz - 1 - g, k, 1:, :] = there[1:]
                o_ref[groups if lowest else gz - g, k, :1, :] = there[:1]

    t_group(0, True)

    def t_step(g, carry):
        t_group(g, False)
        return carry

    lax.fori_loop(1, groups, t_step, 0)


def zt_transform(field, gz, ta):
    _, t, z, _ = field.shape
    field = field.reshape(gz, ta * t, z, N)
    return pl.pallas_call(
        zt_kernel,
        in_specs=[pl.BlockSpec(memory_space=pltpu.VMEM)] * 2,
        out_specs=pl.BlockSpec(memory_space=pltpu.VMEM),
        out_shape=jax.ShapeDtypeStruct((gz, N, z, N), F32),
        scratch_shapes=[pltpu.VMEM((2, gz // 2, N, z, N), F32)],
        compiler_params=pltpu.CompilerParams(vmem_limit_bytes=36 * MIB),
    )(field, jnp.asarray(table_z()))


def join_kernel(x_ref, o_ref, o_buf, o_sem):
    steps, z = o_ref.shape[:2]
    falling = lax.axis_index("gz") >= lax.axis_size("gz") // 2
    lane = lane_of((z, N))
    back = (N + H - lane) % N

    def step(t, carry):
        for i in range(H):
            a, b = x_ref[i, t], x_ref[H + i, t]
            back_a = jnp.take_along_axis(a, back, axis=1)
            back_b = jnp.take_along_axis(b, back, axis=1)
            if i == 0:
                o_buf[t, 0] = jnp.where(lane <= H, a, back_a)
                o_buf[t, H] = jnp.where(lane <= H, b, back_b)
            else:
                o_buf[t, i] = jnp.where(lane < H, a, back_b)
                o_buf[t, N - i] = jnp.where((lane <= H) & (lane > 0), b, back_a)
        for r in range(z):
            pltpu.make_async_copy(
                o_buf.at[t, :, r, :], o_ref.at[t, jnp.where(falling, (z - r) % z, r)], o_sem
            ).start()
        return carry

    lax.fori_loop(0, steps, step, 0)
    pltpu.make_async_copy(o_buf, o_buf, o_sem).wait()


def join(received):
    _, t, z, _ = received.shape
    return pl.pallas_call(
        join_kernel,
        in_specs=[pl.BlockSpec(memory_space=pltpu.VMEM)],
        out_specs=pl.BlockSpec(memory_space=pltpu.HBM),
        out_shape=jax.ShapeDtypeStruct((t, z, N, N), F32),
        scratch_shapes=[pltpu.VMEM((t, N, z, N), F32), pltpu.SemaphoreType.DMA],
        compiler_params=pltpu.CompilerParams(vmem_limit_bytes=20 * MIB),
    )(received)


def body(potential):
    t, z, _, _ = potential.shape
    gz = lax.axis_size("gz")
    ta = lax.axis_size("ta")
    sent = xy_transform(potential)
    field = lax.all_to_all(sent, AXES, split_axis=0, concat_axis=0, tiled=True)
    power = zt_transform(field, gz, ta).reshape(gz * ta, t, z, N)
    received = lax.all_to_all(power, AXES, split_axis=0, concat_axis=0, tiled=True)
    return join(received)


def solution(mesh):
    return jax.shard_map(
        body,
        mesh=mesh,
        in_specs=(P("ta", "gz", None, None),),
        out_specs=P("ta", "gz", None, None),
        check_vma=False,
    )
```

```python
import ml_dtypes
import numpy as np

import jax
import jax.numpy as jnp
from jax import lax
from jax.experimental import pallas as pl
from jax.experimental.pallas import tpu as pltpu
from jax.sharding import PartitionSpec as P

N = 128
H = 64
AXES = ("gz", "ta")
BF = jnp.bfloat16
F32 = jnp.float32
MIB = 2**20
ROOT = float(np.sqrt(0.5))


def split_np(w):
    hi = w.astype(ml_dtypes.bfloat16)
    lo = (w - hi.astype(np.float64)).astype(ml_dtypes.bfloat16)
    return hi, lo


def angles():
    k = np.arange(N)
    phase = np.outer(k, k) % N
    c = np.cos(2 * np.pi * phase / N)
    s = np.sin(2 * np.pi * phase / N)
    quarter = phase % (N // 4) == 0
    c[quarter] = np.round(c[quarter])
    s[quarter] = np.round(s[quarter])
    return c, s


def table_x():
    x = lax.broadcasted_iota(jnp.int32, (N, N), 0)
    lane = lane_of((N, N))
    k = jnp.where(lane <= H, lane, lane - H)
    phase = (x * k + jnp.where(lane > H, N // 4, 0)) % N
    v = (phase - H).astype(F32) * float(np.pi / N)
    v2 = v * v
    sine = jnp.full((N, N), 1.0 / 6227020800.0, F32)
    for c in (-1.0 / 39916800, 1.0 / 362880, -1.0 / 5040, 1.0 / 120, -1.0 / 6, 1.0):
        sine = sine * v2 + c
    sine = sine * v
    hi, lo = split((2.0 * sine * sine - 1.0) * (1.0 / N))
    row = jnp.concatenate([hi, lo], axis=1)
    return jnp.concatenate([row, row], axis=0)


def table_z():
    c, s = angles()
    hi, lo = split_np(np.concatenate([c[: H + 1], s[1:H]], axis=0) / N)
    return np.concatenate([hi, hi, lo, lo], axis=1)


def split(x):
    hi = x.astype(BF)
    lo = (x - hi.astype(F32)).astype(BF)
    return hi, lo


def add(a, b):
    im = b[1] if a[1] is None else a[1] if b[1] is None else a[1] + b[1]
    return a[0] + b[0], im


def sub(a, b):
    im = a[1] if b[1] is None else -b[1] if a[1] is None else a[1] - b[1]
    return a[0] - b[0], im


def turn_by(a, k, n):
    k = k % n
    re, im = a
    if k == 0:
        return a
    if 4 * k == n:
        return jnp.zeros_like(re) if im is None else im, -re
    if im is None:
        angle = 2 * np.pi * k / n
        return re * float(np.cos(angle)), re * float(-np.sin(angle))
    if 8 * k == n:
        return (re + im) * ROOT, (im - re) * ROOT
    if 8 * k == 3 * n:
        return (im - re) * ROOT, (re + im) * -ROOT
    c, s = float(np.cos(2 * np.pi * k / n)), float(np.sin(2 * np.pi * k / n))
    return re * c + im * s, im * c - re * s


def butterfly(a, b, k, n):
    if 4 * k == n and b[1] is not None and a[1] is not None:
        return (a[0] + b[1], a[1] - b[0]), (a[0] - b[1], a[1] + b[0])
    t = turn_by(b, k, n)
    return add(a, t), sub(a, t)


def transform(x):
    n = len(x)
    if n == 1:
        return x
    even, odd = transform(x[0::2]), transform(x[1::2])
    out = [None] * n
    for k in range(n // 2):
        out[k], out[k + n // 2] = butterfly(even[k], odd[k], k, n)
    return out


def transform_real(x):
    n = len(x)
    if n == 1:
        return [(x[0], None)]
    if n == 2:
        return [(x[0] + x[1], None), (x[0] - x[1], None)]
    even, odd = transform_real(x[0::2]), transform_real(x[1::2])
    out = [None] * (n // 2 + 1)
    out[0], out[n // 2] = add(even[0], odd[0]), sub(even[0], odd[0])
    for k in range(1, n // 4):
        (re, im), t = even[k], turn_by(odd[k], k, n)
        out[k], out[n // 2 - k] = (re + t[0], im + t[1]), (re - t[0], t[1] - im)
    out[n // 4] = (even[n // 4][0], -odd[n // 4][0])
    return out


def lane_of(shape):
    return lax.broadcasted_iota(jnp.int32, shape, 1)


def xy_kernel(x_ref, o_ref, w_ref, x_buf, f_buf, h_buf, x_sem):
    steps, planes = x_ref.shape[:2]
    lane = lane_of((planes, N))
    keep = jnp.where(lane == H, 0.0, 1.0).astype(F32)
    turn = jnp.where(lane == 0, 0.0, jnp.where(lane < H, -1.0, 1.0)).astype(F32)
    keep_back = jnp.where(lane == 0, 0.0, 1.0).astype(F32)
    turn_back = jnp.where(lane < H, 1.0, -1.0).astype(F32)
    edge = lane == H

    def fetch(n):
        for z in range(planes):
            pltpu.make_async_copy(
                x_ref.at[pl.ds(2 * n, 2), z], x_buf.at[pl.ds(2 * n, 2), :, z, :], x_sem.at[n]
            ).start()

    for n in range(steps // 2):
        fetch(n)
    w_ref[...] = table_x()

    def step(n, carry):
        whole = x_buf.at[pl.ds(2 * n, 2)]
        pltpu.make_async_copy(whole, whole, x_sem.at[n]).wait()
        for i in range(2):
            plane(2 * n + i)
        return carry

    def plane(t):
        for b in range(8):
            for c, v in enumerate(transform_real([x_buf[t, 8 * a + b] for a in range(16)])):
                re, im = turn_by(v, b * c, N)
                h_buf[0, c, b] = re
                if im is not None:
                    h_buf[1, c, b] = im
        for c in range(9):
            real = c == 0
            parts = []
            for b in range(8):
                flat = real or (c == 8 and b == 0)
                parts.append((h_buf[0, c, b], None if flat else h_buf[1, c, b]))
            if real:
                parts = transform_real([v[0] for v in parts])
            else:
                parts = transform(parts)
            for d, v in enumerate(parts):
                ky = c + 16 * d
                if c == 8 and d >= 4:
                    continue
                re, im = v
                if ky > H:
                    ky, im = N - ky, -im
                f_buf[ky] = re
                if ky % H:
                    f_buf[H + ky] = im

        hi, lo = split(f_buf[...].reshape(N * planes, N))
        r = jnp.dot(jnp.concatenate([hi, lo], axis=1), w_ref[...], preferred_element_type=F32)
        r = (r[:, :N] + r[:, N:]).reshape(N, planes, N)
        o_ref[0, t] = r[0]
        o_ref[H, t] = r[H]
        for i in range(1, H):
            p, q = r[i], r[H + i]
            turned = pltpu.roll(jnp.where(edge, p, q), H, 1)
            o_ref[i, t] = p * keep + turned * turn
            o_ref[H + i, t] = jnp.where(edge, -q, p * keep_back + turned * turn_back)

    lax.fori_loop(0, steps // 2, step, 0)


def xy_transform(potential):
    t, z, _, _ = potential.shape
    return pl.pallas_call(
        xy_kernel,
        in_specs=[pl.BlockSpec(memory_space=pltpu.HBM)],
        out_specs=pl.BlockSpec(memory_space=pltpu.VMEM),
        out_shape=jax.ShapeDtypeStruct((N, t, z, N), F32),
        scratch_shapes=[
            pltpu.VMEM((2 * N, 2 * N), BF),
            pltpu.VMEM((t, N, z, N), F32),
            pltpu.VMEM((N, z, N), F32),
            pltpu.VMEM((2, 9, 8, z, N), F32),
            pltpu.SemaphoreType.DMA((t // 2,)),
        ],
        compiler_params=pltpu.CompilerParams(vmem_limit_bytes=42 * MIB),
    )(potential)


def zt_kernel(x_ref, w_ref, o_ref, y_ref):
    gz, times, planes, _ = x_ref.shape
    groups = gz // 2
    me = lax.axis_index("gz") * lax.axis_size("ta") + lax.axis_index("ta")
    lane = lane_of((1, N))
    first = lane < H
    paired = (me == 0) | (me == H)
    late = me > H
    low, high = lane == 0, lane == H
    u_p = jnp.where(high & late, -1.0, 1.0).astype(F32)
    u_q = jnp.where((low | high) & paired, 0.0, jnp.where(low & late, -1.0, 1.0)).astype(F32)
    v_p = jnp.where((low | high) & paired, 0.0, jnp.where(low & late, -1.0, 1.0)).astype(F32)
    v_q = jnp.where(high & (paired | late), -1.0, 1.0).astype(F32)
    flip = jnp.where((low | high) & late, -1.0, 1.0).astype(F32)
    top = lax.broadcasted_iota(jnp.int32, (planes, N), 0) == 0
    first_8 = lane_of((planes, N)) < H
    edge_8 = (lane_of((planes, N)) == 0) | (lane_of((planes, N)) == H)
    own_8 = edge_8 & paired
    own_top = own_8 & top
    straight = first_8 | own_8

    def z_step(n, carry):
        for m in range(0, 64, 2):
            his, los = zip(*[split(x_ref[:, 64 * n + m + i].reshape(gz * planes, N)) for i in range(2)])
            hi, lo = jnp.concatenate(his, axis=1), jnp.concatenate(los, axis=1)
            out = jnp.dot(w_ref[...], jnp.concatenate([hi, lo, hi, lo], axis=0), preferred_element_type=F32)
            for i in range(2):
                t = 64 * n + m + i
                p, q = out[:H, N * i : N * i + N], out[H:, N * i : N * i + N]
                rp, rq = pltpu.roll(p, H, 1), pltpu.roll(q, H, 1)
                u, v = p * u_p + rq * u_q, rp * v_p - q * v_q
                re, im = jnp.where(first, u, v), jnp.where(first, v, u)
                y_ref[0, :, t] = re.reshape(groups, planes, N)
                y_ref[1, :, t] = im.reshape(groups, planes, N)
                re_0 = jnp.where(first_8, p[:planes], rq[:planes])
                im_0 = jnp.where(first_8, rp[:planes], q[:planes]) * flip
                y_ref[0, 0, t] = jnp.where(top, re_0, re[:planes])
                y_ref[1, 0, t] = jnp.where(top, im_0, im[:planes])
        return carry

    lax.fori_loop(0, times // 64, z_step, 0)

    def t_group(g, lowest):
        for b in range(8):
            parts = transform([(y_ref[0, g, 8 * a + b], y_ref[1, g, 8 * a + b]) for a in range(16)])
            for c, v in enumerate(parts):
                re, im = turn_by(v, b * c, N)
                y_ref[0, g, 8 * c + b] = re
                y_ref[1, g, 8 * c + b] = im
        for c in range(9):
            spectrum = {}
            for k in {c, (16 - c) % 16}:
                parts = transform([(y_ref[0, g, 8 * k + b], y_ref[1, g, 8 * k + b]) for b in range(8)])
                for d, v in enumerate(parts):
                    spectrum[k + 16 * d] = v
            power = {k: re * re + im * im for k, (re, im) in spectrum.items()}
            for k in spectrum:
                ahead, back = power[k], power[(N - k) % N]
                here = jnp.where(straight, ahead, back)
                there = jnp.where(own_8, back, pltpu.roll(jnp.where(first_8, back, ahead), H, 1))
                if lowest:
                    upper = top & ~first_8
                    here, there = jnp.where(upper, there, here), jnp.where(upper, here, there)
                    (re, im), (re_m, im_m) = spectrum[k], spectrum[(N - k) % N]
                    one = (re + re_m) * (re + re_m) + (im - im_m) * (im - im_m)
                    two = (im + im_m) * (im + im_m) + (re - re_m) * (re - re_m)
                    one, two = one * 0.25, two * 0.25
                    mixed = jnp.where(first_8, two, one)
                    mixed = pltpu.roll(mixed, H, 1)
                    here = jnp.where(own_top, jnp.where(first_8, one, mixed), here)
                    there = jnp.where(own_top, jnp.where(first_8, mixed, two), there)
                o_ref[g, k] = here
                o_ref[gz - 1 - g, k, 1:, :] = there[1:]
                o_ref[groups if lowest else gz - g, k, :1, :] = there[:1]

    t_group(0, True)

    def t_step(g, carry):
        t_group(g, False)
        return carry

    lax.fori_loop(1, groups, t_step, 0)


def zt_transform(field, gz, ta):
    _, t, z, _ = field.shape
    field = field.reshape(gz, ta * t, z, N)
    return pl.pallas_call(
        zt_kernel,
        in_specs=[pl.BlockSpec(memory_space=pltpu.VMEM)] * 2,
        out_specs=pl.BlockSpec(memory_space=pltpu.VMEM),
        out_shape=jax.ShapeDtypeStruct((gz, N, z, N), F32),
        scratch_shapes=[pltpu.VMEM((2, gz // 2, N, z, N), F32)],
        compiler_params=pltpu.CompilerParams(vmem_limit_bytes=36 * MIB),
    )(field, jnp.asarray(table_z()))


def join_kernel(x_ref, o_ref, o_buf, o_sem):
    steps, z = o_ref.shape[:2]
    falling = lax.axis_index("gz") >= lax.axis_size("gz") // 2
    lane = lane_of((z, N))
    back = (N + H - lane) % N

    def step(t, carry):
        for i in range(H):
            a, b = x_ref[i, t], x_ref[H + i, t]
            back_a = jnp.take_along_axis(a, back, axis=1)
            back_b = jnp.take_along_axis(b, back, axis=1)
            if i == 0:
                o_buf[t, 0] = jnp.where(lane <= H, a, back_a)
                o_buf[t, H] = jnp.where(lane <= H, b, back_b)
            else:
                o_buf[t, i] = jnp.where(lane < H, a, back_b)
                o_buf[t, N - i] = jnp.where((lane <= H) & (lane > 0), b, back_a)
        for r in range(z):
            pltpu.make_async_copy(
                o_buf.at[t, :, r, :], o_ref.at[t, jnp.where(falling, (z - r) % z, r)], o_sem
            ).start()
        return carry

    lax.fori_loop(0, steps, step, 0)
    pltpu.make_async_copy(o_buf, o_buf, o_sem).wait()


def join(received):
    _, t, z, _ = received.shape
    return pl.pallas_call(
        join_kernel,
        in_specs=[pl.BlockSpec(memory_space=pltpu.VMEM)],
        out_specs=pl.BlockSpec(memory_space=pltpu.HBM),
        out_shape=jax.ShapeDtypeStruct((t, z, N, N), F32),
        scratch_shapes=[pltpu.VMEM((t, N, z, N), F32), pltpu.SemaphoreType.DMA],
        compiler_params=pltpu.CompilerParams(vmem_limit_bytes=20 * MIB),
    )(received)


def body(potential):
    t, z, _, _ = potential.shape
    gz = lax.axis_size("gz")
    ta = lax.axis_size("ta")
    sent = xy_transform(potential)
    field = lax.all_to_all(sent, AXES, split_axis=0, concat_axis=0, tiled=True)
    power = zt_transform(field, gz, ta).reshape(gz * ta, t, z, N)
    received = lax.all_to_all(power, AXES, split_axis=0, concat_axis=0, tiled=True)
    return join(received)


def solution(mesh):
    return jax.shard_map(
        body,
        mesh=mesh,
        in_specs=(P("ta", "gz", None, None),),
        out_specs=P("ta", "gz", None, None),
        check_vma=False,
    )
```

```python
import ml_dtypes
import numpy as np

import jax
import jax.numpy as jnp
from jax import lax
from jax.experimental import pallas as pl
from jax.experimental.pallas import tpu as pltpu
from jax.sharding import PartitionSpec as P

N = 128
H = 64
AXES = ("gz", "ta")
BF = jnp.bfloat16
F32 = jnp.float32
MIB = 2**20
ROOT = float(np.sqrt(0.5))


def split_np(w):
    hi = w.astype(ml_dtypes.bfloat16)
    lo = (w - hi.astype(np.float64)).astype(ml_dtypes.bfloat16)
    return hi, lo


def angles():
    k = np.arange(N)
    phase = np.outer(k, k) % N
    c = np.cos(2 * np.pi * phase / N)
    s = np.sin(2 * np.pi * phase / N)
    quarter = phase % (N // 4) == 0
    c[quarter] = np.round(c[quarter])
    s[quarter] = np.round(s[quarter])
    return c, s


def table_x():
    x = lax.broadcasted_iota(jnp.int32, (N, N), 0)
    lane = lane_of((N, N))
    k = jnp.where(lane <= H, lane, lane - H)
    phase = (x * k + jnp.where(lane > H, N // 4, 0)) % N
    v = (phase - H).astype(F32) * float(np.pi / N)
    v2 = v * v
    sine = jnp.full((N, N), 1.0 / 6227020800.0, F32)
    for c in (-1.0 / 39916800, 1.0 / 362880, -1.0 / 5040, 1.0 / 120, -1.0 / 6, 1.0):
        sine = sine * v2 + c
    sine = sine * v
    hi, lo = split((2.0 * sine * sine - 1.0) * (1.0 / N))
    row = jnp.concatenate([hi, lo], axis=1)
    return jnp.concatenate([row, row], axis=0)


def table_z():
    c, s = angles()
    hi, lo = split_np(np.concatenate([c[: H + 1], s[1:H]], axis=0) / N)
    return np.concatenate([hi, hi, lo, lo], axis=1)


def split(x):
    hi = x.astype(BF)
    lo = (x - hi.astype(F32)).astype(BF)
    return hi, lo


def add(a, b):
    im = b[1] if a[1] is None else a[1] if b[1] is None else a[1] + b[1]
    return a[0] + b[0], im


def sub(a, b):
    im = a[1] if b[1] is None else -b[1] if a[1] is None else a[1] - b[1]
    return a[0] - b[0], im


def turn_by(a, k, n):
    k = k % n
    re, im = a
    if k == 0:
        return a
    if 4 * k == n:
        return jnp.zeros_like(re) if im is None else im, -re
    if im is None:
        angle = 2 * np.pi * k / n
        return re * float(np.cos(angle)), re * float(-np.sin(angle))
    if 8 * k == n:
        return (re + im) * ROOT, (im - re) * ROOT
    if 8 * k == 3 * n:
        return (im - re) * ROOT, (re + im) * -ROOT
    c, s = float(np.cos(2 * np.pi * k / n)), float(np.sin(2 * np.pi * k / n))
    return re * c + im * s, im * c - re * s


def butterfly(a, b, k, n):
    if 4 * k == n and b[1] is not None and a[1] is not None:
        return (a[0] + b[1], a[1] - b[0]), (a[0] - b[1], a[1] + b[0])
    t = turn_by(b, k, n)
    return add(a, t), sub(a, t)


def transform(x):
    n = len(x)
    if n == 1:
        return x
    even, odd = transform(x[0::2]), transform(x[1::2])
    out = [None] * n
    for k in range(n // 2):
        out[k], out[k + n // 2] = butterfly(even[k], odd[k], k, n)
    return out


def transform_real(x):
    n = len(x)
    if n == 1:
        return [(x[0], None)]
    if n == 2:
        return [(x[0] + x[1], None), (x[0] - x[1], None)]
    even, odd = transform_real(x[0::2]), transform_real(x[1::2])
    out = [None] * (n // 2 + 1)
    out[0], out[n // 2] = add(even[0], odd[0]), sub(even[0], odd[0])
    for k in range(1, n // 4):
        (re, im), t = even[k], turn_by(odd[k], k, n)
        out[k], out[n // 2 - k] = (re + t[0], im + t[1]), (re - t[0], t[1] - im)
    out[n // 4] = (even[n // 4][0], -odd[n // 4][0])
    return out


def lane_of(shape):
    return lax.broadcasted_iota(jnp.int32, shape, 1)


def xy_kernel(x_ref, o_ref, w_ref, x_buf, f_bufs, h_bufs, x_sem):
    steps, planes = x_ref.shape[:2]
    lane = lane_of((planes, N))
    keep = jnp.where(lane == H, 0.0, 1.0).astype(F32)
    turn = jnp.where(lane == 0, 0.0, jnp.where(lane < H, -1.0, 1.0)).astype(F32)
    keep_back = jnp.where(lane == 0, 0.0, 1.0).astype(F32)
    turn_back = jnp.where(lane < H, 1.0, -1.0).astype(F32)
    edge = lane == H

    def fetch(n):
        for z in range(planes):
            pltpu.make_async_copy(
                x_ref.at[pl.ds(2 * n, 2), z], x_buf.at[pl.ds(2 * n, 2), :, z, :], x_sem.at[n]
            ).start()

    for n in range(steps // 2):
        fetch(n)
    w_ref[...] = table_x()

    def step(n, carry):
        whole = x_buf.at[pl.ds(2 * n, 2)]
        pltpu.make_async_copy(whole, whole, x_sem.at[n]).wait()
        for i in range(2):
            plane(2 * n + i, f_bufs.at[i], h_bufs.at[i])
        return carry

    def plane(t, f_buf, h_buf):
        for b in range(8):
            for c, v in enumerate(transform_real([x_buf[t, 8 * a + b] for a in range(16)])):
                re, im = turn_by(v, b * c, N)
                h_buf[0, c, b] = re
                if im is not None:
                    h_buf[1, c, b] = im
        for c in range(9):
            real = c == 0
            parts = []
            for b in range(8):
                flat = real or (c == 8 and b == 0)
                parts.append((h_buf[0, c, b], None if flat else h_buf[1, c, b]))
            if real:
                parts = transform_real([v[0] for v in parts])
            else:
                parts = transform(parts)
            for d, v in enumerate(parts):
                ky = c + 16 * d
                if c == 8 and d >= 4:
                    continue
                re, im = v
                if ky > H:
                    ky, im = N - ky, -im
                f_buf[ky] = re
                if ky % H:
                    f_buf[H + ky] = im

        hi, lo = split(f_buf[...].reshape(N * planes, N))
        r = jnp.dot(jnp.concatenate([hi, lo], axis=1), w_ref[...], preferred_element_type=F32)
        r = (r[:, :N] + r[:, N:]).reshape(N, planes, N)
        o_ref[0, t] = r[0]
        o_ref[H, t] = r[H]
        for i in range(1, H):
            p, q = r[i], r[H + i]
            turned = pltpu.roll(jnp.where(edge, p, q), H, 1)
            o_ref[i, t] = p * keep + turned * turn
            o_ref[H + i, t] = jnp.where(edge, -q, p * keep_back + turned * turn_back)

    lax.fori_loop(0, steps // 2, step, 0)


def xy_transform(potential):
    t, z, _, _ = potential.shape
    return pl.pallas_call(
        xy_kernel,
        in_specs=[pl.BlockSpec(memory_space=pltpu.HBM)],
        out_specs=pl.BlockSpec(memory_space=pltpu.VMEM),
        out_shape=jax.ShapeDtypeStruct((N, t, z, N), F32),
        scratch_shapes=[
            pltpu.VMEM((2 * N, 2 * N), BF),
            pltpu.VMEM((t, N, z, N), F32),
            pltpu.VMEM((2, N, z, N), F32),
            pltpu.VMEM((2, 2, 9, 8, z, N), F32),
            pltpu.SemaphoreType.DMA((t // 2,)),
        ],
        compiler_params=pltpu.CompilerParams(vmem_limit_bytes=42 * MIB),
    )(potential)


def zt_kernel(x_ref, w_ref, o_ref, y_ref):
    gz, times, planes, _ = x_ref.shape
    groups = gz // 2
    me = lax.axis_index("gz") * lax.axis_size("ta") + lax.axis_index("ta")
    lane = lane_of((1, N))
    first = lane < H
    paired = (me == 0) | (me == H)
    late = me > H
    low, high = lane == 0, lane == H
    u_p = jnp.where(high & late, -1.0, 1.0).astype(F32)
    u_q = jnp.where((low | high) & paired, 0.0, jnp.where(low & late, -1.0, 1.0)).astype(F32)
    v_p = jnp.where((low | high) & paired, 0.0, jnp.where(low & late, -1.0, 1.0)).astype(F32)
    v_q = jnp.where(high & (paired | late), -1.0, 1.0).astype(F32)
    flip = jnp.where((low | high) & late, -1.0, 1.0).astype(F32)
    top = lax.broadcasted_iota(jnp.int32, (planes, N), 0) == 0
    first_8 = lane_of((planes, N)) < H
    edge_8 = (lane_of((planes, N)) == 0) | (lane_of((planes, N)) == H)
    own_8 = edge_8 & paired
    own_top = own_8 & top
    straight = first_8 | own_8

    def z_step(n, carry):
        for m in range(0, 64, 2):
            his, los = zip(*[split(x_ref[:, 64 * n + m + i].reshape(gz * planes, N)) for i in range(2)])
            hi, lo = jnp.concatenate(his, axis=1), jnp.concatenate(los, axis=1)
            out = jnp.dot(w_ref[...], jnp.concatenate([hi, lo, hi, lo], axis=0), preferred_element_type=F32)
            for i in range(2):
                t = 64 * n + m + i
                p, q = out[:H, N * i : N * i + N], out[H:, N * i : N * i + N]
                rp, rq = pltpu.roll(p, H, 1), pltpu.roll(q, H, 1)
                u, v = p * u_p + rq * u_q, rp * v_p - q * v_q
                re, im = jnp.where(first, u, v), jnp.where(first, v, u)
                y_ref[0, :, t] = re.reshape(groups, planes, N)
                y_ref[1, :, t] = im.reshape(groups, planes, N)
                re_0 = jnp.where(first_8, p[:planes], rq[:planes])
                im_0 = jnp.where(first_8, rp[:planes], q[:planes]) * flip
                y_ref[0, 0, t] = jnp.where(top, re_0, re[:planes])
                y_ref[1, 0, t] = jnp.where(top, im_0, im[:planes])
        return carry

    lax.fori_loop(0, times // 64, z_step, 0)

    def t_group(g, lowest):
        for b in range(8):
            parts = transform([(y_ref[0, g, 8 * a + b], y_ref[1, g, 8 * a + b]) for a in range(16)])
            for c, v in enumerate(parts):
                re, im = turn_by(v, b * c, N)
                y_ref[0, g, 8 * c + b] = re
                y_ref[1, g, 8 * c + b] = im
        for c in range(9):
            spectrum = {}
            for k in {c, (16 - c) % 16}:
                parts = transform([(y_ref[0, g, 8 * k + b], y_ref[1, g, 8 * k + b]) for b in range(8)])
                for d, v in enumerate(parts):
                    spectrum[k + 16 * d] = v
            power = {k: re * re + im * im for k, (re, im) in spectrum.items()}
            for k in spectrum:
                ahead, back = power[k], power[(N - k) % N]
                here = jnp.where(straight, ahead, back)
                there = jnp.where(own_8, back, pltpu.roll(jnp.where(first_8, back, ahead), H, 1))
                if lowest:
                    upper = top & ~first_8
                    here, there = jnp.where(upper, there, here), jnp.where(upper, here, there)
                    (re, im), (re_m, im_m) = spectrum[k], spectrum[(N - k) % N]
                    one = (re + re_m) * (re + re_m) + (im - im_m) * (im - im_m)
                    two = (im + im_m) * (im + im_m) + (re - re_m) * (re - re_m)
                    one, two = one * 0.25, two * 0.25
                    mixed = jnp.where(first_8, two, one)
                    mixed = pltpu.roll(mixed, H, 1)
                    here = jnp.where(own_top, jnp.where(first_8, one, mixed), here)
                    there = jnp.where(own_top, jnp.where(first_8, mixed, two), there)
                o_ref[g, k] = here
                o_ref[gz - 1 - g, k, 1:, :] = there[1:]
                o_ref[groups if lowest else gz - g, k, :1, :] = there[:1]

    t_group(0, True)

    def t_step(g, carry):
        t_group(2 * g + 1, False)
        t_group(2 * g + 2, False)
        return carry

    lax.fori_loop(0, groups // 2 - 1, t_step, 0)
    t_group(groups - 1, False)


def zt_transform(field, gz, ta):
    _, t, z, _ = field.shape
    field = field.reshape(gz, ta * t, z, N)
    return pl.pallas_call(
        zt_kernel,
        in_specs=[pl.BlockSpec(memory_space=pltpu.VMEM)] * 2,
        out_specs=pl.BlockSpec(memory_space=pltpu.VMEM),
        out_shape=jax.ShapeDtypeStruct((gz, N, z, N), F32),
        scratch_shapes=[pltpu.VMEM((2, gz // 2, N, z, N), F32)],
        compiler_params=pltpu.CompilerParams(vmem_limit_bytes=36 * MIB),
    )(field, jnp.asarray(table_z()))


def join_kernel(x_ref, o_ref, o_buf, o_sem):
    steps, z = o_ref.shape[:2]
    falling = lax.axis_index("gz") >= lax.axis_size("gz") // 2
    lane = lane_of((z, N))
    back = (N + H - lane) % N

    def step(t, carry):
        for i in range(H):
            a, b = x_ref[i, t], x_ref[H + i, t]
            back_a = jnp.take_along_axis(a, back, axis=1)
            back_b = jnp.take_along_axis(b, back, axis=1)
            if i == 0:
                o_buf[t, 0] = jnp.where(lane <= H, a, back_a)
                o_buf[t, H] = jnp.where(lane <= H, b, back_b)
            else:
                o_buf[t, i] = jnp.where(lane < H, a, back_b)
                o_buf[t, N - i] = jnp.where((lane <= H) & (lane > 0), b, back_a)
        for r in range(z):
            pltpu.make_async_copy(
                o_buf.at[t, :, r, :], o_ref.at[t, jnp.where(falling, (z - r) % z, r)], o_sem
            ).start()
        return carry

    lax.fori_loop(0, steps, step, 0)
    pltpu.make_async_copy(o_buf, o_buf, o_sem).wait()


def join(received):
    _, t, z, _ = received.shape
    return pl.pallas_call(
        join_kernel,
        in_specs=[pl.BlockSpec(memory_space=pltpu.VMEM)],
        out_specs=pl.BlockSpec(memory_space=pltpu.HBM),
        out_shape=jax.ShapeDtypeStruct((t, z, N, N), F32),
        scratch_shapes=[pltpu.VMEM((t, N, z, N), F32), pltpu.SemaphoreType.DMA],
        compiler_params=pltpu.CompilerParams(vmem_limit_bytes=20 * MIB),
    )(received)


def body(potential):
    t, z, _, _ = potential.shape
    gz = lax.axis_size("gz")
    ta = lax.axis_size("ta")
    sent = xy_transform(potential)
    field = lax.all_to_all(sent, AXES, split_axis=0, concat_axis=0, tiled=True)
    power = zt_transform(field, gz, ta).reshape(gz * ta, t, z, N)
    received = lax.all_to_all(power, AXES, split_axis=0, concat_axis=0, tiled=True)
    return join(received)


def solution(mesh):
    return jax.shard_map(
        body,
        mesh=mesh,
        in_specs=(P("ta", "gz", None, None),),
        out_specs=P("ta", "gz", None, None),
        check_vma=False,
    )
```
